128 devices in a mesh: users: 8 (over y, core), items: 16 (over z, x).
Axes of the slice: x: 4, y: 4, z: 4, core: 2. Of those that a mesh axis runs over, the one named last changes fastest.
Arguments:
- user_factors: bfloat16 [64, 128, 256], P('users'), may hold values from -1.5 to 1.5
- item_factors: bfloat16 [128, 128, 256], P('items'), may hold values from -1.5 to 1.5
- confidence: bfloat16 [128, 256, 128, 128], P(('users', 'items')), may hold values from 0.25 to 4
- ratings: bfloat16 [128, 256, 128, 128], P(('users', 'items')), may hold values from -6 to 6
- slot_blocks: int32 [128, 16, 2], P(('users', 'items')), may hold values from -1 to 7, as said below
- pair_user: int32 [128, 256], P(('users', 'items')), may hold values from 0 to 7
- pair_slot: int32 [128, 256], P(('users', 'items')), may hold values from 0 to 31, as said below
Outputs:
- user_gradient: float32 [64, 128, 256], P('users')
- item_gradient: float32 [128, 128, 256], P('items')
The draws below stay inside these ranges and needn't reach their ends.
Inputs may be any that keep to these rules, and one draw needn't show every extreme that they name: `slot_blocks`: each device lists from each owner between 1 and 2 distinct live blocks of 0 to 7, in the first slots, the rest -1. In every draw each row of devices along items lists 2 blocks of one owner from every device, and some slot is empty. `pair_slot`: every pair names a live slot.
All inputs are finite; a program needn't handle non-finite values.
Results may differ from the reference program's by a relative error of at most 0.00045.
Values may be sent and summed in bfloat16 or wider, within the bound.
No kernel may reach another device: no remote copies, remote signals or barrier semaphores. Data moves between devices by JAX's collectives and lax.ppermute only.
A program may use at most 128 MiB of HBM per device.

```python
import math
import jax
import jax.numpy as jnp
from jax import lax

R = 256
BLK = 128
UB_DEV = 8
IB_DEV = 8
CAP = 2
PAIRS = 256
NUB = 64
NIB = 128
N_USERS = 8
N_ITEMS = 16
DEVICES = 128


def shared_lists(key):
    key_count, key_hot, key_perm, key_owner, key_within = jax.random.split(key, 5)
    counts = jax.random.randint(key_count, (DEVICES, N_ITEMS), 1, CAP + 1)
    hot_owner = jnp.repeat(jax.random.randint(key_hot, (N_USERS,), 0, N_ITEMS), N_ITEMS)
    columns = jnp.arange(N_ITEMS)[None, :]
    counts = jnp.where(columns == ((hot_owner + 1) % N_ITEMS)[:, None], 1, counts)
    counts = jnp.where(columns == hot_owner[:, None], CAP, counts)
    key_list = jax.random.split(key_perm, DEVICES * N_ITEMS)

    def shuffle(single):
        return jax.random.permutation(single, IB_DEV)[:CAP]
    shuffled = jax.vmap(shuffle)(key_list).reshape(DEVICES, N_ITEMS, CAP).astype(jnp.int32)
    live = jnp.arange(CAP)[None, None, :] < counts[:, :, None]
    slot_blocks = jnp.where(live, shuffled, -1).astype(jnp.int32)
    owner_pick = jax.random.randint(key_owner, (DEVICES, PAIRS), 0, N_ITEMS)
    chosen = jnp.take_along_axis(counts, owner_pick, axis=1)
    within = jax.random.randint(key_within, (DEVICES, PAIRS), 0, 1048576) % chosen
    pair_slot = (owner_pick * CAP + within).astype(jnp.int32)
    return (slot_blocks, pair_slot)


def draw_slot_blocks(key, part):
    return shared_lists(key)[0]


def draw_pair_slot(key, part):
    return shared_lists(key)[1]


def with_ends(drawn, rng, smallest, top_value):
    shape = drawn.shape
    place = [jax.random.randint(jax.random.fold_in(rng, axis), (), 0, shape[axis]) for axis in range(len(shape))]
    drawn = drawn.at[tuple(place)].set(smallest)
    longest = shape.index(max(shape))
    place[longest] = (place[longest] + 1) % shape[longest]
    return drawn.at[tuple(place)].set(top_value)


def steps_of(key, shape, pieces, least, largest):
    gain = 1.0
    for dim, parts in pieces:
        steps = jax.random.uniform(jax.random.fold_in(jax.random.fold_in(key, 6), dim), (parts,), jnp.float32, least / len(pieces), largest / len(pieces))
        gain = gain * jnp.repeat(jnp.exp(steps), shape[dim] // parts).reshape((-1,) + (1,) * (len(shape) - 1 - dim))
    return gain


def normal_values(stream_key, extent, spread, most, cuts=(), held_as=jnp.bfloat16):
    gain = steps_of(stream_key, extent, cuts, -0.22, 0.18) if cuts else 1.0
    result = jax.random.normal(stream_key, extent, jnp.float32) * spread * gain
    return jnp.minimum(jnp.maximum(result, -most), most).astype(held_as)


def setup_inputs(seed: int = 0) -> dict:
    arg_keys = jax.random.split(jax.random.key(seed), 8)
    user_factors = normal_values(arg_keys[0], (NUB, BLK, R), (R ** 0.5) ** -0.5, 1.5, ((0, 8),))
    item_factors = normal_values(arg_keys[1], (NIB, BLK, R), (R ** 0.5) ** -0.5, 1.5, ((0, 16),))
    confidence = jnp.clip(jnp.exp(math.log(4.0) - 2.7725887 * jax.random.uniform(arg_keys[2], (DEVICES, PAIRS, BLK, BLK), jnp.float32) ** steps_of(arg_keys[2], (DEVICES, PAIRS, BLK, BLK), ((0, 128),), -0.2, 0.2)), 0.25, 4.0).astype(jnp.bfloat16)
    ratings = normal_values(arg_keys[3], (DEVICES, PAIRS, BLK, BLK), 1.0, 6.0, ((0, 128),))
    slot_blocks = draw_slot_blocks(jax.random.fold_in(arg_keys[7], 71), 0)
    pair_user = with_ends(jax.random.randint(arg_keys[5], (DEVICES, PAIRS), 0, UB_DEV), jax.random.fold_in(arg_keys[5], 1), 0, UB_DEV - 1).astype(jnp.int32)
    pair_slot = draw_pair_slot(jax.random.fold_in(arg_keys[7], 71), 0)
    return dict(user_factors=user_factors, item_factors=item_factors, confidence=confidence, ratings=ratings, slot_blocks=slot_blocks, pair_user=pair_user, pair_slot=pair_slot)


def reference(user_factors, item_factors, confidence, ratings, slot_blocks, pair_user, pair_slot):
    devices = jnp.arange(DEVICES, dtype=jnp.int32)
    user_index = (devices // N_ITEMS)[:, None] * UB_DEV + pair_user
    owner_index = pair_slot // CAP
    local_ids = jnp.take_along_axis(slot_blocks.reshape(DEVICES, N_ITEMS * CAP), pair_slot, axis=1)
    item_index = (owner_index * IB_DEV + local_ids).astype(jnp.int32)

    def advance(carry, inputs):
        acc_user, acc_item = carry
        conf_tile, rate_tile, user_rows, item_rows = inputs
        left_tile = user_factors[user_rows].astype(jnp.float32)
        right_tile = item_factors[item_rows].astype(jnp.float32)
        scores = jnp.einsum("pir,pjr->pij", left_tile, right_tile)
        weighted = (conf_tile.astype(jnp.float32) * (scores - rate_tile.astype(jnp.float32)) / BLK).astype(jnp.bfloat16)
        weighted = lax.optimization_barrier(weighted).astype(jnp.float32)
        acc_user = acc_user.at[user_rows].add(jnp.einsum("pij,pjr->pir", weighted, right_tile))
        acc_item = acc_item.at[item_rows].add(jnp.einsum("pij,pir->pjr", weighted, left_tile))
        return (acc_user, acc_item), None

    start = (jnp.zeros(user_factors.shape, jnp.float32), jnp.zeros(item_factors.shape, jnp.float32))
    (user_gradient, item_gradient), _ = lax.scan(advance, start, (confidence, ratings, user_index, item_index))
    return user_gradient, item_gradient
```

```python
import jax
import jax.numpy as jnp
from jax import lax
from jax.experimental import pallas as pl
from jax.experimental.pallas import tpu as pltpu
from jax.sharding import PartitionSpec as P

F32 = jnp.float32
I16 = jnp.int16
I32 = jnp.int32
META = 16
STEP = 16
LIMIT = 60 * 1024 * 1024


def params():
    return pltpu.CompilerParams(vmem_limit_bytes=LIMIT)


def vmem():
    return pl.BlockSpec(memory_space=pltpu.VMEM)


def smem():
    return pl.BlockSpec(memory_space=pltpu.SMEM)


def encode(x):
    top = jnp.max(jnp.abs(x), axis=0, keepdims=True)
    expo = jnp.ceil(jnp.log2(jnp.maximum(top, 1e-30)) + 1e-4)
    scaled = x * jnp.exp2(14.99 - expo)
    codes = jnp.clip(jnp.round(scaled), -32767.0, 32767.0)
    return codes.astype(I32).astype(I16), expo.astype(I32)


def decode(codes, expo):
    return codes.astype(I32).astype(F32) * jnp.exp2(expo.astype(F32) - 14.99)


def meta_rows(rows):
    width = rows[0].shape[1]
    index = lax.broadcasted_iota(I32, (META, width), 0)
    out = jnp.zeros((META, width), I32)
    for k, row in enumerate(rows):
        out = jnp.where(index == k, row, out)
    return out.astype(I16)


def pick_kernel(ids, blocks, out):
    for i in range(out.shape[0]):
        for q in range(out.shape[1]):
            out[i, q] = blocks[jnp.maximum(ids[i, q], 0)]


def pair_kernel(pu, ps, wanted, conf, rate, users, slots, msg, ugrad, sgrad):
    step = pl.program_id(0)
    count = conf.shape[0]
    tile = conf.shape[1]

    @pl.when(step == 0)
    def _():
        ugrad[...] = jnp.zeros_like(ugrad)
        sgrad[...] = jnp.zeros_like(sgrad)

    for k in range(count):
        b = pu[step * count + k]
        s = ps[step * count + k]
        left = users[b]
        right = slots[s]
        score = lax.dot_general(left, right, (((1,), (1,)), ((), ())), preferred_element_type=F32)
        weighted = (
            conf[k].astype(F32) * (score - rate[k].astype(F32)) * (1.0 / tile)
        ).astype(jnp.bfloat16)
        ugrad[b] += lax.dot_general(
            weighted, right, (((1,), (0,)), ((), ())), preferred_element_type=F32
        )
        sgrad[s] += lax.dot_general(
            weighted, left, (((0,), (0,)), ((), ())), preferred_element_type=F32
        )

    @pl.when(step == pl.num_programs(0) - 1)
    def _():
        owners = msg.shape[0]
        cap = sgrad.shape[0] // owners
        part = (msg.shape[1] - META) - cap * tile
        per = tile // part
        for i in range(owners):
            rows = []
            for q in range(cap):
                codes, expo = encode(sgrad[i * cap + q])
                msg[i, q * tile : (q + 1) * tile] = codes
                rows.append(expo)
            chunk = ugrad[i // per, (i % per) * part : (i % per + 1) * part]
            codes, expo = encode(chunk)
            msg[i, cap * tile : cap * tile + part] = codes
            rows.append(expo)
            msg[i, cap * tile + part :] = meta_rows(rows)


def owner_kernel(ids, got, imsg, umsg, acc):
    owners = got.shape[0]
    held, tile, width = acc.shape
    cap = ids.shape[1]
    part = (got.shape[1] - META) - cap * tile
    acc[...] = jnp.zeros_like(acc)
    total = jnp.zeros((part, width), F32)
    for i in range(owners):
        meta = got[i, cap * tile + part :].astype(I32)
        for q in range(cap):
            block = ids[i, q]
            value = decode(got[i, q * tile : (q + 1) * tile], meta[q : q + 1])

            @pl.when(block >= 0)
            def _():
                acc[block] += value

        total += decode(got[i, cap * tile : cap * tile + part], meta[cap : cap + 1])
    for r in range(held):
        codes, expo = encode(acc[r])
        imsg[r, :tile] = codes
        imsg[r, tile:] = meta_rows([expo])
    codes, expo = encode(total)
    meta = meta_rows([expo])
    for i in range(owners):
        umsg[i, :part] = codes
        umsg[i, part:] = meta


def sum_kernel(got, msg):
    tile = got.shape[1] - META
    total = jnp.zeros((tile, got.shape[2]), F32)
    for r in range(got.shape[0]):
        meta = got[r, tile:].astype(I32)
        total += decode(got[r, :tile], meta[0:1])
    codes, expo = encode(total)
    meta = meta_rows([expo])
    for r in range(got.shape[0]):
        msg[r, :tile] = codes
        msg[r, tile:] = meta


def spread_kernel(got, out):
    part = got.shape[1] - META
    per = out.shape[1] // part
    for r in range(got.shape[0]):
        meta = got[r, part:].astype(I32)
        out[r // per, (r % per) * part : (r % per + 1) * part] = decode(got[r, :part], meta[0:1])


def body(user_factors, item_factors, confidence, ratings, slot_blocks, pair_user, pair_slot):
    owners = lax.axis_size("items")
    rows = lax.axis_size("users")
    held, tile, width = item_factors.shape
    cap = slot_blocks.shape[2]
    count = pair_user.shape[1]
    part = user_factors.shape[0] * tile // owners
    step = min(STEP, count)
    wanted = slot_blocks[0]

    asked = lax.all_to_all(wanted, "items", 0, 0, tiled=True)
    outgoing = pl.pallas_call(
        pick_kernel,
        out_shape=jax.ShapeDtypeStruct((owners, cap, tile, width), item_factors.dtype),
        in_specs=[smem(), vmem()],
        out_specs=vmem(),
        compiler_params=params(),
        name="pick",
    )(asked, item_factors)
    incoming = lax.all_to_all(outgoing, "items", 0, 0, tiled=True)
    slots = incoming.reshape(owners * cap, tile, width)

    depth = cap * tile + part + META
    msg = pl.pallas_call(
        pair_kernel,
        out_shape=jax.ShapeDtypeStruct((owners, depth, width), I16),
        grid_spec=pltpu.PrefetchScalarGridSpec(
            num_scalar_prefetch=3,
            grid=(count // step,),
            in_specs=[
                pl.BlockSpec((step, tile, tile), lambda p, *_: (p, 0, 0)),
                pl.BlockSpec((step, tile, tile), lambda p, *_: (p, 0, 0)),
                vmem(),
                vmem(),
            ],
            out_specs=vmem(),
            scratch_shapes=[
                pltpu.VMEM(user_factors.shape, F32),
                pltpu.VMEM((owners * cap, tile, width), F32),
            ],
        ),
        compiler_params=params(),
        name="pairs",
    )(pair_user[0], pair_slot[0], wanted, confidence[0], ratings[0], user_factors, slots)

    back = lax.all_to_all(msg, "items", 0, 0, tiled=True)
    imsg, umsg = pl.pallas_call(
        owner_kernel,
        out_shape=(
            jax.ShapeDtypeStruct((rows, tile + META, width), I16),
            jax.ShapeDtypeStruct((owners, part + META, width), I16),
        ),
        in_specs=[smem(), vmem()],
        out_specs=(vmem(), vmem()),
        scratch_shapes=[pltpu.VMEM(item_factors.shape, F32)],
        compiler_params=params(),
        name="owners",
    )(asked, back)

    igot = lax.all_to_all(imsg, "users", 0, 0, tiled=True)
    ugot = lax.all_to_all(umsg, "items", 0, 0, tiled=True)
    isum = pl.pallas_call(
        sum_kernel,
        out_shape=jax.ShapeDtypeStruct(igot.shape, I16),
        in_specs=[vmem()],
        out_specs=vmem(),
        compiler_params=params(),
        name="sums",
    )(igot)
    iall = lax.all_to_all(isum, "users", 0, 0, tiled=True)

    def spread(got, shape, name):
        return pl.pallas_call(
            spread_kernel,
            out_shape=jax.ShapeDtypeStruct(shape, F32),
            in_specs=[vmem()],
            out_specs=vmem(),
            compiler_params=params(),
            name=name,
        )(got)

    return (
        spread(ugot, user_factors.shape, "spread_users"),
        spread(iall, item_factors.shape, "spread_items"),
    )


def solution(mesh):
    in_specs = (
        P("users", None, None),
        P("items", None, None),
        P(("users", "items"), None, None, None),
        P(("users", "items"), None, None, None),
        P(("users", "items"), None, None),
        P(("users", "items"), None),
        P(("users", "items"), None),
    )
    out_specs = (P("users", None, None), P("items", None, None))
    return jax.shard_map(body, mesh=mesh, in_specs=in_specs, out_specs=out_specs, check_vma=False)
```

```python
import jax
import jax.numpy as jnp
from jax import lax
from jax.experimental import pallas as pl
from jax.experimental.pallas import tpu as pltpu
from jax.sharding import PartitionSpec as P

F32 = jnp.float32
I16 = jnp.int16
I32 = jnp.int32
META = 16
STEP = 32
GROUP = 8
LIMIT = 60 * 1024 * 1024


def params():
    return pltpu.CompilerParams(vmem_limit_bytes=LIMIT)


def vmem():
    return pl.BlockSpec(memory_space=pltpu.VMEM)


def smem():
    return pl.BlockSpec(memory_space=pltpu.SMEM)


def encode(x):
    top = jnp.max(jnp.abs(x), axis=0, keepdims=True)
    expo = jnp.ceil(jnp.log2(jnp.maximum(top, 1e-30)) + 1e-4)
    scaled = x * jnp.exp2(14.99 - expo)
    codes = jnp.clip(jnp.round(scaled), -32767.0, 32767.0)
    return codes.astype(I32).astype(I16), expo.astype(I32)


def decode(codes, expo):
    return codes.astype(I32).astype(F32) * jnp.exp2(expo.astype(F32) - 14.99)


def meta_rows(rows):
    width = rows[0].shape[1]
    index = lax.broadcasted_iota(I32, (META, width), 0)
    out = jnp.zeros((META, width), I32)
    for k, row in enumerate(rows):
        out = jnp.where(index == k, row, out)
    return out.astype(I16)


def dot(x, y, i, j):
    return lax.dot_general(x, y, (((i,), (j,)), ((), ())), preferred_element_type=F32)


def pick_kernel(ids, blocks, out):
    for i in range(out.shape[0]):
        for q in range(out.shape[1]):
            out[i, q] = blocks[jnp.maximum(ids[i, q], 0)]


def pair_kernel(pu, ps, wanted, conf, rate, users, slots, msg, ugrad, sgrad):
    step = pl.program_id(0)
    count = conf.shape[0]
    tile = conf.shape[1]

    @pl.when(step == 0)
    def _():
        ugrad[...] = jnp.zeros_like(ugrad)
        sgrad[...] = jnp.zeros_like(sgrad)

    for base in range(0, count, GROUP):
        picks = range(base, base + GROUP)
        bs = [pu[step * count + k] for k in picks]
        ss = [ps[step * count + k] for k in picks]
        lefts = [users[b] for b in bs]
        rights = [slots[s] for s in ss]
        scores = [dot(x, y, 1, 1) for x, y in zip(lefts, rights)]
        tiles = [
            (conf[k].astype(F32) * (score - rate[k].astype(F32)) * (1.0 / tile)).astype(jnp.bfloat16)
            for k, score in zip(picks, scores)
        ]
        by_user = [dot(w, y, 1, 0) for w, y in zip(tiles, rights)]
        by_slot = [dot(w, x, 0, 0) for w, x in zip(tiles, lefts)]
        for b, s, x, y in zip(bs, ss, by_user, by_slot):
            ugrad[b] += x
            sgrad[s] += y

    @pl.when(step == pl.num_programs(0) - 1)
    def _():
        owners = msg.shape[0]
        cap = sgrad.shape[0] // owners
        part = (msg.shape[1] - META) - cap * tile
        per = tile // part
        for i in range(owners):
            rows = []
            for q in range(cap):
                codes, expo = encode(sgrad[i * cap + q])
                msg[i, q * tile : (q + 1) * tile] = codes
                rows.append(expo)
            chunk = ugrad[i // per, (i % per) * part : (i % per + 1) * part]
            codes, expo = encode(chunk)
            msg[i, cap * tile : cap * tile + part] = codes
            rows.append(expo)
            msg[i, cap * tile + part :] = meta_rows(rows)


def owner_kernel(place, ids, got, keep, give, umsg, acc):
    owners = got.shape[0]
    held, tile, width = acc.shape
    half = held // 2
    cap = ids.shape[1]
    part = (got.shape[1] - META) - cap * tile
    acc[...] = jnp.zeros_like(acc)
    total = jnp.zeros((part, width), F32)
    for i in range(owners):
        meta = got[i, cap * tile + part :].astype(I32)
        for q in range(cap):
            block = ids[i, q]
            value = decode(got[i, q * tile : (q + 1) * tile], meta[q : q + 1])

            @pl.when(block >= 0)
            def _():
                acc[block] += value

        total += decode(got[i, cap * tile : cap * tile + part], meta[cap : cap + 1])
    core = place[0]
    for r in range(half):
        keep[r] = acc[core * half + r]
        give[r] = acc[(1 - core) * half + r]
    codes, expo = encode(total)
    meta = meta_rows([expo])
    for i in range(owners):
        umsg[i, :part] = codes
        umsg[i, part:] = meta


def chip_kernel(keep, got, msg):
    tile = keep.shape[1]
    for r in range(keep.shape[0]):
        codes, expo = encode(keep[r] + got[r])
        msg[r, :tile] = codes
        msg[r, tile:] = meta_rows([expo])


def ring_kernel(place, own, one, two, three, out, stack):
    half, tile, _ = out.shape
    chips = stack.shape[0]
    for r in range(half):
        for k, ref in enumerate((own, one, two, three)):
            meta = ref[r, tile:].astype(I32)
            stack[k] = decode(ref[r, :tile], meta[0:1])
        total = stack[lax.rem(place[1], chips)]
        for y in range(1, chips):
            total += stack[lax.rem(place[1] + chips - y, chips)]
        out[r] = total


def join_kernel(place, mine, other, out):
    half = mine.shape[0]
    core = place[0]
    for r in range(half):
        out[core * half + r] = mine[r]
        out[(1 - core) * half + r] = other[r]


def spread_kernel(got, out):
    part = got.shape[1] - META
    per = out.shape[1] // part
    for r in range(got.shape[0]):
        meta = got[r, part:].astype(I32)
        out[r // per, (r % per) * part : (r % per + 1) * part] = decode(got[r, :part], meta[0:1])


def body(user_factors, item_factors, confidence, ratings, slot_blocks, pair_user, pair_slot):
    owners = lax.axis_size("items")
    rows = lax.axis_size("users")
    held, tile, width = item_factors.shape
    cap = slot_blocks.shape[2]
    count = pair_user.shape[1]
    part = user_factors.shape[0] * tile // owners
    step = min(STEP, count)
    wanted = slot_blocks[0]

    asked = lax.all_to_all(wanted, "items", 0, 0, tiled=True)
    outgoing = pl.pallas_call(
        pick_kernel,
        out_shape=jax.ShapeDtypeStruct((owners, cap, tile, width), item_factors.dtype),
        in_specs=[smem(), vmem()],
        out_specs=vmem(),
        compiler_params=params(),
        name="pick",
    )(asked, item_factors)
    incoming = lax.all_to_all(outgoing, "items", 0, 0, tiled=True)
    slots = incoming.reshape(owners * cap, tile, width)

    depth = cap * tile + part + META
    msg = pl.pallas_call(
        pair_kernel,
        out_shape=jax.ShapeDtypeStruct((owners, depth, width), I16),
        grid_spec=pltpu.PrefetchScalarGridSpec(
            num_scalar_prefetch=3,
            grid=(count // step,),
            in_specs=[
                pl.BlockSpec((step, tile, tile), lambda p, *_: (p, 0, 0)),
                pl.BlockSpec((step, tile, tile), lambda p, *_: (p, 0, 0)),
                vmem(),
                vmem(),
            ],
            out_specs=vmem(),
            scratch_shapes=[
                pltpu.VMEM(user_factors.shape, F32),
                pltpu.VMEM((owners * cap, tile, width), F32),
            ],
        ),
        compiler_params=params(),
        name="pairs",
    )(pair_user[0], pair_slot[0], wanted, confidence[0], ratings[0], user_factors, slots)

    back = lax.all_to_all(msg, "items", 0, 0, tiled=True)
    half = (held // 2, tile, width)
    row = lax.axis_index("users")
    place = jnp.stack([row % 2, row // 2]).astype(I32)
    keep, give, umsg = pl.pallas_call(
        owner_kernel,
        out_shape=(
            jax.ShapeDtypeStruct(half, F32),
            jax.ShapeDtypeStruct(half, F32),
            jax.ShapeDtypeStruct((owners, part + META, width), I16),
        ),
        in_specs=[smem(), smem(), vmem()],
        out_specs=(vmem(), vmem(), vmem()),
        scratch_shapes=[pltpu.VMEM(item_factors.shape, F32)],
        compiler_params=params(),
        name="owners",
    )(place, asked, back)

    swap = [(u, u ^ 1) for u in range(rows)]
    mate = lax.ppermute(give, "users", swap)
    code = pl.pallas_call(
        chip_kernel,
        out_shape=jax.ShapeDtypeStruct((held // 2, tile + META, width), I16),
        in_specs=[vmem(), vmem()],
        out_specs=vmem(),
        compiler_params=params(),
        name="chip",
    )(keep, mate)
    code, umsg = lax.optimization_barrier((code, umsg))
    ring = [
        lax.ppermute(code, "users", [(u, (u + 2 * k) % rows) for u in range(rows)])
        for k in range(1, 4)
    ]
    ugot = lax.all_to_all(umsg, "items", 0, 0, tiled=True)
    mine = pl.pallas_call(
        ring_kernel,
        out_shape=jax.ShapeDtypeStruct(half, F32),
        in_specs=[smem()] + [vmem()] * 4,
        out_specs=vmem(),
        scratch_shapes=[pltpu.VMEM((4, tile, width), F32)],
        compiler_params=params(),
        name="ring",
    )(place, code, *ring)
    other = lax.ppermute(mine, "users", swap)
    item_total = pl.pallas_call(
        join_kernel,
        out_shape=jax.ShapeDtypeStruct(item_factors.shape, F32),
        in_specs=[smem(), vmem(), vmem()],
        out_specs=vmem(),
        compiler_params=params(),
        name="join",
    )(place, mine, other)
    user_total = pl.pallas_call(
        spread_kernel,
        out_shape=jax.ShapeDtypeStruct(user_factors.shape, F32),
        in_specs=[vmem()],
        out_specs=vmem(),
        compiler_params=params(),
        name="spread",
    )(ugot)
    return user_total, item_total


def solution(mesh):
    in_specs = (
        P("users", None, None),
        P("items", None, None),
        P(("users", "items"), None, None, None),
        P(("users", "items"), None, None, None),
        P(("users", "items"), None, None),
        P(("users", "items"), None),
        P(("users", "items"), None),
    )
    out_specs = (P("users", None, None), P("items", None, None))
    return jax.shard_map(body, mesh=mesh, in_specs=in_specs, out_specs=out_specs, check_vma=False)
```

```python
import jax
import jax.numpy as jnp
from jax import lax
from jax.experimental import pallas as pl
from jax.experimental.pallas import tpu as pltpu
from jax.sharding import PartitionSpec as P

F32 = jnp.float32
I16 = jnp.int16
I32 = jnp.int32
META = 16
STEP = 32
GROUP = 8
LIMIT = 32 * 1024 * 1024


def params():
    return pltpu.CompilerParams(vmem_limit_bytes=LIMIT)


def vmem():
    return pl.BlockSpec(memory_space=pltpu.VMEM)


def near(x):
    return pltpu.with_memory_space_constraint(x, pltpu.VMEM)


def far(x):
    return pltpu.with_memory_space_constraint(x, pltpu.HBM)


def made(shape, dtype):
    return pltpu.VMEM(shape, dtype)


def smem():
    return pl.BlockSpec(memory_space=pltpu.SMEM)


def encode(x):
    top = jnp.max(jnp.abs(x), axis=0, keepdims=True)
    expo = jnp.ceil(jnp.log2(jnp.maximum(top, 1e-30)) + 1e-4)
    scaled = x * jnp.exp2(14.99 - expo)
    codes = jnp.clip(jnp.round(scaled), -32767.0, 32767.0)
    return codes.astype(I32).astype(I16), expo.astype(I32)


def decode(codes, expo):
    return codes.astype(I32).astype(F32) * jnp.exp2(expo.astype(F32) - 14.99)


def meta_rows(rows):
    width = rows[0].shape[1]
    index = lax.broadcasted_iota(I32, (META, width), 0)
    out = jnp.zeros((META, width), I32)
    for k, row in enumerate(rows):
        out = jnp.where(index == k, row, out)
    return out.astype(I16)


def dot(x, y, i, j):
    return lax.dot_general(x, y, (((i,), (j,)), ((), ())), preferred_element_type=F32)


def pick_kernel(ids, blocks, out):
    for i in range(out.shape[0]):
        for q in range(out.shape[1]):
            out[i, q] = blocks[jnp.maximum(ids[i, q], 0)]


def pair_kernel(pu, ps, wanted, conf, rate, users, slots, msg, ugrad, sgrad):
    step = pl.program_id(0)
    count = conf.shape[0]
    tile = conf.shape[1]

    @pl.when(step == 0)
    def _():
        ugrad[...] = jnp.zeros_like(ugrad)
        sgrad[...] = jnp.zeros_like(sgrad)

    for base in range(0, count, GROUP):
        picks = range(base, base + GROUP)
        bs = [pu[step * count + k] for k in picks]
        ss = [ps[step * count + k] for k in picks]
        lefts = [users[b] for b in bs]
        rights = [slots[s] for s in ss]
        scores = [dot(x, y, 1, 1) for x, y in zip(lefts, rights)]
        tiles = [
            (conf[k].astype(F32) * (score - rate[k].astype(F32)) * (1.0 / tile)).astype(jnp.bfloat16)
            for k, score in zip(picks, scores)
        ]
        by_user = [dot(w, y, 1, 0) for w, y in zip(tiles, rights)]
        by_slot = [dot(w, x, 0, 0) for w, x in zip(tiles, lefts)]
        for b, s, x, y in zip(bs, ss, by_user, by_slot):
            ugrad[b] += x
            sgrad[s] += y

    @pl.when(step == pl.num_programs(0) - 1)
    def _():
        owners = msg.shape[0]
        cap = sgrad.shape[0] // owners
        part = (msg.shape[1] - META) - cap * tile
        per = tile // part
        for i in range(owners):
            rows = []
            for q in range(cap):
                codes, expo = encode(sgrad[i * cap + q])
                msg[i, q * tile : (q + 1) * tile] = codes
                rows.append(expo)
            chunk = ugrad[i // per, (i % per) * part : (i % per + 1) * part]
            codes, expo = encode(chunk)
            msg[i, cap * tile : cap * tile + part] = codes
            rows.append(expo)
            msg[i, cap * tile + part :] = meta_rows(rows)


def owner_kernel(place, ids, got, keep, give, umsg, acc):
    owners = got.shape[0]
    held, tile, width = acc.shape
    half = held // 2
    cap = ids.shape[1]
    part = (got.shape[1] - META) - cap * tile
    acc[...] = jnp.zeros_like(acc)
    total = jnp.zeros((part, width), F32)
    for i in range(owners):
        meta = got[i, cap * tile + part :].astype(I32)
        for q in range(cap):
            block = ids[i, q]
            value = decode(got[i, q * tile : (q + 1) * tile], meta[q : q + 1])

            @pl.when(block >= 0)
            def _():
                acc[block] += value

        total += decode(got[i, cap * tile : cap * tile + part], meta[cap : cap + 1])
    core = place[0]
    for r in range(half):
        keep[r] = acc[core * half + r]
        give[r] = acc[(1 - core) * half + r]
    codes, expo = encode(total)
    meta = meta_rows([expo])
    for i in range(owners):
        umsg[i, :part] = codes
        umsg[i, part:] = meta


def chip_kernel(keep, got, msg):
    tile = keep.shape[1]
    for r in range(keep.shape[0]):
        codes, expo = encode(keep[r] + got[r])
        msg[r, :tile] = codes
        msg[r, tile:] = meta_rows([expo])


def ring_kernel(place, own, one, two, three, out, stack):
    half, tile, _ = out.shape
    chips = stack.shape[0]
    for r in range(half):
        for k, ref in enumerate((own, one, two, three)):
            meta = ref[r, tile:].astype(I32)
            stack[k] = decode(ref[r, :tile], meta[0:1])
        total = stack[lax.rem(place[1], chips)]
        for y in range(1, chips):
            total += stack[lax.rem(place[1] + chips - y, chips)]
        out[r] = total


def join_kernel(place, mine, other, out):
    half = mine.shape[0]
    core = place[0]
    for r in range(half):
        out[core * half + r] = mine[r]
        out[(1 - core) * half + r] = other[r]


def spread_kernel(got, out):
    part = got.shape[1] - META
    per = out.shape[1] // part
    for r in range(got.shape[0]):
        meta = got[r, part:].astype(I32)
        out[r // per, (r % per) * part : (r % per + 1) * part] = decode(got[r, :part], meta[0:1])


def body(user_factors, item_factors, confidence, ratings, slot_blocks, pair_user, pair_slot):
    owners = lax.axis_size("items")
    rows = lax.axis_size("users")
    held, tile, width = item_factors.shape
    cap = slot_blocks.shape[2]
    count = pair_user.shape[1]
    part = user_factors.shape[0] * tile // owners
    step = min(STEP, count)
    wanted = slot_blocks[0]

    asked = lax.all_to_all(wanted, "items", 0, 0, tiled=True)
    outgoing = pl.pallas_call(
        pick_kernel,
        out_shape=pltpu.HBM((owners, cap, tile, width), item_factors.dtype),
        in_specs=[smem(), vmem()],
        out_specs=vmem(),
        compiler_params=params(),
        name="pick",
    )(asked, item_factors)
    incoming = lax.all_to_all(outgoing, "items", 0, 0, tiled=True)
    slots = near(incoming.reshape(owners * cap, tile, width))

    depth = cap * tile + part + META
    msg = pl.pallas_call(
        pair_kernel,
        out_shape=pltpu.HBM((owners, depth, width), I16),
        grid_spec=pltpu.PrefetchScalarGridSpec(
            num_scalar_prefetch=3,
            grid=(count // step,),
            in_specs=[
                pl.BlockSpec((step, tile, tile), lambda p, *_: (p, 0, 0)),
                pl.BlockSpec((step, tile, tile), lambda p, *_: (p, 0, 0)),
                vmem(),
                vmem(),
            ],
            out_specs=vmem(),
            scratch_shapes=[
                pltpu.VMEM(user_factors.shape, F32),
                pltpu.VMEM((owners * cap, tile, width), F32),
            ],
        ),
        compiler_params=params(),
        name="pairs",
    )(pair_user[0], pair_slot[0], wanted, far(confidence[0]), far(ratings[0]), user_factors, slots)

    back = lax.all_to_all(msg, "items", 0, 0, tiled=True)
    half = (held // 2, tile, width)
    row = lax.axis_index("users")
    place = jnp.stack([row % 2, row // 2]).astype(I32)
    keep, give, umsg = pl.pallas_call(
        owner_kernel,
        out_shape=(
            made(half, F32),
            made(half, F32),
            pltpu.HBM((owners, part + META, width), I16),
        ),
        in_specs=[smem(), smem(), vmem()],
        out_specs=(vmem(), vmem(), vmem()),
        scratch_shapes=[pltpu.VMEM(item_factors.shape, F32)],
        compiler_params=params(),
        name="owners",
    )(place, asked, near(back))

    swap = [(u, u ^ 1) for u in range(rows)]
    mate = lax.ppermute(give, "users", swap)
    code = pl.pallas_call(
        chip_kernel,
        out_shape=made((held // 2, tile + META, width), I16),
        in_specs=[vmem(), vmem()],
        out_specs=vmem(),
        compiler_params=params(),
        name="chip",
    )(near(keep), near(mate))
    code, umsg = lax.optimization_barrier((code, umsg))
    ring = [
        lax.ppermute(code, "users", [(u, (u + 2 * k) % rows) for u in range(rows)])
        for k in range(1, 4)
    ]
    ugot = lax.all_to_all(umsg, "items", 0, 0, tiled=True)
    mine = pl.pallas_call(
        ring_kernel,
        out_shape=made(half, F32),
        in_specs=[smem()] + [vmem()] * 4,
        out_specs=vmem(),
        scratch_shapes=[pltpu.VMEM((4, tile, width), F32)],
        compiler_params=params(),
        name="ring",
    )(place, near(code), *[near(x) for x in ring])
    other = lax.ppermute(mine, "users", swap)
    item_total = pl.pallas_call(
        join_kernel,
        out_shape=jax.ShapeDtypeStruct(item_factors.shape, F32),
        in_specs=[smem(), vmem(), vmem()],
        out_specs=vmem(),
        compiler_params=params(),
        name="join",
    )(place, near(mine), near(other))
    user_total = pl.pallas_call(
        spread_kernel,
        out_shape=jax.ShapeDtypeStruct(user_factors.shape, F32),
        in_specs=[vmem()],
        out_specs=vmem(),
        compiler_params=params(),
        name="spread",
    )(near(ugot))
    return user_total, item_total


def solution(mesh):
    in_specs = (
        P("users", None, None),
        P("items", None, None),
        P(("users", "items"), None, None, None),
        P(("users", "items"), None, None, None),
        P(("users", "items"), None, None),
        P(("users", "items"), None),
        P(("users", "items"), None),
    )
    out_specs = (P("users", None, None), P("items", None, None))
    return jax.shard_map(body, mesh=mesh, in_specs=in_specs, out_specs=out_specs, check_vma=False)
```

```python
import functools

import jax
import jax.numpy as jnp
from jax import lax
from jax.experimental import pallas as pl
from jax.experimental.pallas import tpu as pltpu
from jax.sharding import PartitionSpec as P

F32 = jnp.float32
I16 = jnp.int16
I32 = jnp.int32
META = 16
STEP = 32
GROUP = 8
LIMIT = 32 * 1024 * 1024


def params():
    return pltpu.CompilerParams(vmem_limit_bytes=LIMIT)


def vmem():
    return pl.BlockSpec(memory_space=pltpu.VMEM)


def near(x):
    return pltpu.with_memory_space_constraint(x, pltpu.VMEM)


def far(x):
    return pltpu.with_memory_space_constraint(x, pltpu.HBM)


def made(shape, dtype):
    return pltpu.VMEM(shape, dtype)


def hbm():
    return pl.BlockSpec(memory_space=pl.ANY)


def smem():
    return pl.BlockSpec(memory_space=pltpu.SMEM)


def encode(x):
    top = jnp.max(jnp.abs(x), axis=0, keepdims=True)
    expo = jnp.ceil(jnp.log2(jnp.maximum(top, 1e-30)) + 1e-4)
    scaled = x * jnp.exp2(14.99 - expo)
    codes = jnp.clip(jnp.round(scaled), -32767.0, 32767.0)
    return codes.astype(I32).astype(I16), expo.astype(I32)


def decode(codes, expo):
    return codes.astype(I32).astype(F32) * jnp.exp2(expo.astype(F32) - 14.99)


def meta_rows(rows):
    width = rows[0].shape[1]
    index = lax.broadcasted_iota(I32, (META, width), 0)
    out = jnp.zeros((META, width), I32)
    for k, row in enumerate(rows):
        out = jnp.where(index == k, row, out)
    return out.astype(I16)


def dot(x, y, i, j):
    return lax.dot_general(x, y, (((i,), (j,)), ((), ())), preferred_element_type=F32)


def pick_kernel(ids, blocks, out, sems):
    copies = []
    for i in range(out.shape[0]):
        for q in range(out.shape[1]):
            block = jnp.maximum(ids[i, q], 0)
            copies.append(pltpu.make_async_copy(blocks.at[block], out.at[i, q], sems.at[i, q]))
            copies[-1].start()
    for copy in copies:
        copy.wait()


def pair_kernel(pu, ps, conf, rate, users, slots, out, ugrad, sgrad, msg, sems):
    step = pl.program_id(0)
    count = conf.shape[0]
    tile = conf.shape[1]

    @pl.when(step == 0)
    def _():
        ugrad[...] = jnp.zeros_like(ugrad)
        sgrad[...] = jnp.zeros_like(sgrad)

    for base in range(0, count, GROUP):
        picks = range(base, base + GROUP)
        bs = [pu[step * count + k] for k in picks]
        ss = [ps[step * count + k] for k in picks]
        lefts = [users[b] for b in bs]
        rights = [slots[s] for s in ss]
        scores = [dot(x, y, 1, 1) for x, y in zip(lefts, rights)]
        tiles = [
            (conf[k].astype(F32) * (score - rate[k].astype(F32)) * (1.0 / tile)).astype(jnp.bfloat16)
            for k, score in zip(picks, scores)
        ]
        by_user = [dot(w, y, 1, 0) for w, y in zip(tiles, rights)]
        by_slot = [dot(w, x, 0, 0) for w, x in zip(tiles, lefts)]
        for b, s, x, y in zip(bs, ss, by_user, by_slot):
            ugrad[b] += x
            sgrad[s] += y

    @pl.when(step == pl.num_programs(0) - 1)
    def _():
        owners = msg.shape[0]
        cap = sgrad.shape[0] // owners
        part = (msg.shape[1] - META) - cap * tile
        per = tile // part
        copies = []
        for i in range(owners):
            rows = []
            for q in range(cap):
                codes, expo = encode(sgrad[i * cap + q])
                msg[i, q * tile : (q + 1) * tile] = codes
                rows.append(expo)
            chunk = ugrad[i // per, (i % per) * part : (i % per + 1) * part]
            codes, expo = encode(chunk)
            msg[i, cap * tile : cap * tile + part] = codes
            rows.append(expo)
            msg[i, cap * tile + part :] = meta_rows(rows)
            copies.append(pltpu.make_async_copy(msg.at[i], out.at[i], sems.at[i]))
            copies[-1].start()
        for copy in copies:
            copy.wait()


def item_kernel(place, ids, got, keep, give, acc):
    owners = got.shape[0]
    held, tile, width = acc.shape
    half = held // 2
    cap = ids.shape[1]
    part = (got.shape[1] - META) - cap * tile
    acc[...] = jnp.zeros_like(acc)
    for i in range(owners):
        meta = got[i, cap * tile + part :].astype(I32)
        for q in range(cap):
            block = ids[i, q]
            value = decode(got[i, q * tile : (q + 1) * tile], meta[q : q + 1])

            @pl.when(block >= 0)
            def _():
                acc[block] += value

    core = place[0]
    for r in range(half):
        keep[r] = acc[core * half + r]
        give[r] = acc[(1 - core) * half + r]


def user_kernel(cap, got, umsg):
    owners, rows, width = umsg.shape
    part = rows - META
    first = got.shape[1] - META - part
    total = jnp.zeros((part, width), F32)
    for i in range(owners):
        meta = got[i, first + part :].astype(I32)
        total += decode(got[i, first : first + part], meta[cap : cap + 1])
    codes, expo = encode(total)
    meta = meta_rows([expo])
    for i in range(owners):
        umsg[i, :part] = codes
        umsg[i, part:] = meta


def chip_kernel(keep, got, msg):
    half, tile, _ = keep.shape
    rows = []
    for r in range(half):
        codes, expo = encode(keep[r] + got[r])
        msg[r * tile : (r + 1) * tile] = codes
        rows.append(expo)
    msg[half * tile :] = meta_rows(rows)


def ring_kernel(place, own, one, two, three, out, stack):
    half, tile, _ = out.shape
    chips = stack.shape[0]
    for r in range(half):
        for k, ref in enumerate((own, one, two, three)):
            meta = ref[half * tile :].astype(I32)
            stack[k] = decode(ref[r * tile : (r + 1) * tile], meta[r : r + 1])
        total = stack[lax.rem(place[1], chips)]
        for y in range(1, chips):
            total += stack[lax.rem(place[1] + chips - y, chips)]
        out[r] = total


def join_kernel(place, mine, other, out):
    half = mine.shape[0]
    core = place[0]
    for r in range(half):
        out[core * half + r] = mine[r]
        out[(1 - core) * half + r] = other[r]


def spread_kernel(got, out):
    part = got.shape[1] - META
    per = out.shape[1] // part
    for r in range(got.shape[0]):
        meta = got[r, part:].astype(I32)
        out[r // per, (r % per) * part : (r % per + 1) * part] = decode(got[r, :part], meta[0:1])


def body(user_factors, item_factors, confidence, ratings, slot_blocks, pair_user, pair_slot):
    owners = lax.axis_size("items")
    rows = lax.axis_size("users")
    held, tile, width = item_factors.shape
    cap = slot_blocks.shape[2]
    count = pair_user.shape[1]
    part = user_factors.shape[0] * tile // owners
    step = min(STEP, count)
    wanted = slot_blocks[0]

    asked = lax.all_to_all(wanted, "items", 0, 0, tiled=True)
    outgoing = pl.pallas_call(
        pick_kernel,
        out_shape=pltpu.HBM((owners, cap, tile, width), item_factors.dtype),
        in_specs=[smem(), hbm()],
        out_specs=hbm(),
        scratch_shapes=[pltpu.SemaphoreType.DMA((owners, cap))],
        compiler_params=params(),
        name="pick",
    )(asked, far(item_factors))
    incoming = lax.all_to_all(outgoing, "items", 0, 0, tiled=True)
    slots = near(incoming.reshape(owners * cap, tile, width))

    depth = cap * tile + part + META
    msg = pl.pallas_call(
        pair_kernel,
        out_shape=pltpu.HBM((owners, depth, width), I16),
        grid_spec=pltpu.PrefetchScalarGridSpec(
            num_scalar_prefetch=2,
            grid=(count // step,),
            in_specs=[
                pl.BlockSpec((step, tile, tile), lambda p, *_: (p, 0, 0)),
                pl.BlockSpec((step, tile, tile), lambda p, *_: (p, 0, 0)),
                vmem(),
                vmem(),
            ],
            out_specs=hbm(),
            scratch_shapes=[
                pltpu.VMEM(user_factors.shape, F32),
                pltpu.VMEM((owners * cap, tile, width), F32),
                pltpu.VMEM((owners, depth, width), I16),
                pltpu.SemaphoreType.DMA((owners,)),
            ],
        ),
        compiler_params=params(),
        name="pairs",
    )(pair_user[0], pair_slot[0], far(confidence[0]), far(ratings[0]), user_factors, slots)

    back = lax.all_to_all(msg, "items", 0, 0, tiled=True)
    half = (held // 2, tile, width)
    row = lax.axis_index("users")
    place = jnp.stack([row % 2, row // 2]).astype(I32)
    keep, give = pl.pallas_call(
        item_kernel,
        out_shape=(made(half, F32), made(half, F32)),
        in_specs=[smem(), smem(), vmem()],
        out_specs=(vmem(), vmem()),
        scratch_shapes=[pltpu.VMEM(item_factors.shape, F32)],
        compiler_params=params(),
        name="owners",
    )(place, asked, near(back))

    swap = [(u, u ^ 1) for u in range(rows)]
    back, give = lax.optimization_barrier((back, give))
    mate = lax.ppermute(give, "users", swap)
    umsg = pl.pallas_call(
        functools.partial(user_kernel, cap),
        out_shape=pltpu.HBM((owners, part + META, width), I16),
        in_specs=[vmem()],
        out_specs=vmem(),
        compiler_params=params(),
        name="users",
    )(near(back))
    keep, umsg = lax.optimization_barrier((keep, umsg))
    code = pl.pallas_call(
        chip_kernel,
        out_shape=made((held // 2 * tile + META, width), I16),
        in_specs=[vmem(), vmem()],
        out_specs=vmem(),
        compiler_params=params(),
        name="chip",
    )(near(keep), near(mate))
    ring = [
        lax.ppermute(code, "users", [(u, (u + 2 * k) % rows) for u in range(rows)])
        for k in range(1, 4)
    ]
    ugot = lax.all_to_all(umsg, "items", 0, 0, tiled=True)
    mine = pl.pallas_call(
        ring_kernel,
        out_shape=made(half, F32),
        in_specs=[smem()] + [vmem()] * 4,
        out_specs=vmem(),
        scratch_shapes=[pltpu.VMEM((4, tile, width), F32)],
        compiler_params=params(),
        name="ring",
    )(place, near(code), *[near(x) for x in ring])
    other = lax.ppermute(mine, "users", swap)
    item_total = pl.pallas_call(
        join_kernel,
        out_shape=jax.ShapeDtypeStruct(item_factors.shape, F32),
        in_specs=[smem(), vmem(), vmem()],
        out_specs=vmem(),
        compiler_params=params(),
        name="join",
    )(place, near(mine), near(other))
    user_total = pl.pallas_call(
        spread_kernel,
        out_shape=jax.ShapeDtypeStruct(user_factors.shape, F32),
        in_specs=[vmem()],
        out_specs=vmem(),
        compiler_params=params(),
        name="spread",
    )(near(ugot))
    return user_total, item_total


def solution(mesh):
    in_specs = (
        P("users", None, None),
        P("items", None, None),
        P(("users", "items"), None, None, None),
        P(("users", "items"), None, None, None),
        P(("users", "items"), None, None),
        P(("users", "items"), None),
        P(("users", "items"), None),
    )
    out_specs = (P("users", None, None), P("items", None, None))
    return jax.shard_map(body, mesh=mesh, in_specs=in_specs, out_specs=out_specs, check_vma=False)
```

```python
import functools

import jax
import jax.numpy as jnp
from jax import lax
from jax.experimental import pallas as pl
from jax.experimental.pallas import tpu as pltpu
from jax.sharding import PartitionSpec as P

F32 = jnp.float32
I16 = jnp.int16
I32 = jnp.int32
META = 16
STEP = 32
GROUP = 8
LIMIT = 32 * 1024 * 1024


def params():
    return pltpu.CompilerParams(vmem_limit_bytes=LIMIT)


def vmem():
    return pl.BlockSpec(memory_space=pltpu.VMEM)


def near(x):
    return pltpu.with_memory_space_constraint(x, pltpu.VMEM)


def far(x):
    return pltpu.with_memory_space_constraint(x, pltpu.HBM)


def made(shape, dtype):
    return pltpu.VMEM(shape, dtype)


def smem():
    return pl.BlockSpec(memory_space=pltpu.SMEM)


def encode(x):
    top = jnp.max(jnp.abs(x), axis=0, keepdims=True)
    expo = jnp.ceil(jnp.log2(jnp.maximum(top, 1e-30)) + 1e-4)
    scaled = x * jnp.exp2(14.99 - expo)
    codes = jnp.clip(jnp.round(scaled), -32767.0, 32767.0)
    return codes.astype(I32).astype(I16), expo.astype(I32)


def decode(codes, expo):
    return codes.astype(I32).astype(F32) * jnp.exp2(expo.astype(F32) - 14.99)


def meta_rows(rows):
    width = rows[0].shape[1]
    index = lax.broadcasted_iota(I32, (META, width), 0)
    out = jnp.zeros((META, width), I32)
    for k, row in enumerate(rows):
        out = jnp.where(index == k, row, out)
    return out.astype(I16)


def dot(x, y, i, j):
    return lax.dot_general(x, y, (((i,), (j,)), ((), ())), preferred_element_type=F32)


def pick_kernel(ids, blocks, out):
    for i in range(out.shape[0]):
        for q in range(out.shape[1]):
            out[i, q] = blocks[jnp.maximum(ids[i, q], 0)]


def pair_kernel(pu, ps, conf, rate, users, slots, msg, ugrad, sgrad):
    step = pl.program_id(0)
    count = conf.shape[0]
    tile = conf.shape[1]

    @pl.when(step == 0)
    def _():
        ugrad[...] = jnp.zeros_like(ugrad)
        sgrad[...] = jnp.zeros_like(sgrad)

    for base in range(0, count, GROUP):
        picks = range(base, base + GROUP)
        bs = [pu[step * count + k] for k in picks]
        ss = [ps[step * count + k] for k in picks]
        lefts = [users[b] for b in bs]
        rights = [slots[s] for s in ss]
        scores = [dot(x, y, 1, 1) for x, y in zip(lefts, rights)]
        tiles = [
            (conf[k].astype(F32) * (score - rate[k].astype(F32)) * (1.0 / tile)).astype(jnp.bfloat16)
            for k, score in zip(picks, scores)
        ]
        by_user = [dot(w, y, 1, 0) for w, y in zip(tiles, rights)]
        by_slot = [dot(w, x, 0, 0) for w, x in zip(tiles, lefts)]
        for b, s, x, y in zip(bs, ss, by_user, by_slot):
            ugrad[b] += x
            sgrad[s] += y

    @pl.when(step == pl.num_programs(0) - 1)
    def _():
        owners = msg.shape[0]
        cap = sgrad.shape[0] // owners
        part = (msg.shape[1] - META) - cap * tile
        per = tile // part
        for i in range(owners):
            rows = []
            for q in range(cap):
                codes, expo = encode(sgrad[i * cap + q])
                msg[i, q * tile : (q + 1) * tile] = codes
                rows.append(expo)
            chunk = ugrad[i // per, (i % per) * part : (i % per + 1) * part]
            codes, expo = encode(chunk)
            msg[i, cap * tile : cap * tile + part] = codes
            rows.append(expo)
            msg[i, cap * tile + part :] = meta_rows(rows)


def item_kernel(place, ids, got, keep, give, acc):
    owners = got.shape[0]
    held, tile, width = acc.shape
    half = held // 2
    cap = ids.shape[1]
    part = (got.shape[1] - META) - cap * tile
    acc[...] = jnp.zeros_like(acc)
    for i in range(owners):
        meta = got[i, cap * tile + part :].astype(I32)
        for q in range(cap):
            block = ids[i, q]
            value = decode(got[i, q * tile : (q + 1) * tile], meta[q : q + 1])

            @pl.when(block >= 0)
            def _():
                acc[block] += value

    core = place[0]
    for r in range(half):
        keep[r] = acc[core * half + r]
        give[r] = acc[(1 - core) * half + r]


def user_kernel(cap, got, umsg):
    owners, rows, width = umsg.shape
    part = rows - META
    first = got.shape[1] - META - part
    total = jnp.zeros((part, width), F32)
    for i in range(owners):
        meta = got[i, first + part :].astype(I32)
        total += decode(got[i, first : first + part], meta[cap : cap + 1])
    codes, expo = encode(total)
    meta = meta_rows([expo])
    for i in range(owners):
        umsg[i, :part] = codes
        umsg[i, part:] = meta


def chip_kernel(keep, got, msg):
    half, tile, _ = keep.shape
    rows = []
    for r in range(half):
        codes, expo = encode(keep[r] + got[r])
        msg[r * tile : (r + 1) * tile] = codes
        rows.append(expo)
    msg[half * tile :] = meta_rows(rows)


def ring_kernel(place, own, one, two, three, out, stack):
    half, tile, _ = out.shape
    chips = stack.shape[0]
    for r in range(half):
        for k, ref in enumerate((own, one, two, three)):
            meta = ref[half * tile :].astype(I32)
            stack[k] = decode(ref[r * tile : (r + 1) * tile], meta[r : r + 1])
        total = stack[lax.rem(place[1], chips)]
        for y in range(1, chips):
            total += stack[lax.rem(place[1] + chips - y, chips)]
        out[r] = total


def join_kernel(place, mine, other, out):
    half = mine.shape[0]
    core = place[0]
    for r in range(half):
        out[core * half + r] = mine[r]
        out[(1 - core) * half + r] = other[r]


def spread_kernel(got, out):
    part = got.shape[1] - META
    per = out.shape[1] // part
    for r in range(got.shape[0]):
        meta = got[r, part:].astype(I32)
        out[r // per, (r % per) * part : (r % per + 1) * part] = decode(got[r, :part], meta[0:1])


def body(user_factors, item_factors, confidence, ratings, slot_blocks, pair_user, pair_slot):
    owners = lax.axis_size("items")
    rows = lax.axis_size("users")
    held, tile, width = item_factors.shape
    cap = slot_blocks.shape[2]
    count = pair_user.shape[1]
    part = user_factors.shape[0] * tile // owners
    step = min(STEP, count)
    row = lax.axis_index("users").astype(I32)
    place = jnp.stack([row & 1, row >> 1])
    wanted, place = lax.optimization_barrier((slot_blocks[0], place))

    asked = lax.all_to_all(wanted, "items", 0, 0, tiled=True)
    outgoing = pl.pallas_call(
        pick_kernel,
        out_shape=made((owners, cap, tile, width), item_factors.dtype),
        in_specs=[smem(), vmem()],
        out_specs=vmem(),
        compiler_params=params(),
        name="pick",
    )(asked, near(item_factors))
    incoming = lax.all_to_all(outgoing, "items", 0, 0, tiled=True)
    slots = near(incoming.reshape(owners * cap, tile, width))

    depth = cap * tile + part + META
    msg = pl.pallas_call(
        pair_kernel,
        out_shape=made((owners, depth, width), I16),
        grid_spec=pltpu.PrefetchScalarGridSpec(
            num_scalar_prefetch=2,
            grid=(count // step,),
            in_specs=[
                pl.BlockSpec((step, tile, tile), lambda p, *_: (p, 0, 0)),
                pl.BlockSpec((step, tile, tile), lambda p, *_: (p, 0, 0)),
                vmem(),
                vmem(),
            ],
            out_specs=vmem(),
            scratch_shapes=[
                pltpu.VMEM(user_factors.shape, F32),
                pltpu.VMEM((owners * cap, tile, width), F32),
            ],
        ),
        compiler_params=params(),
        name="pairs",
    )(pair_user[0], pair_slot[0], far(confidence[0]), far(ratings[0]), user_factors, slots)

    back = lax.all_to_all(msg, "items", 0, 0, tiled=True)
    half = (held // 2, tile, width)
    keep, give = pl.pallas_call(
        item_kernel,
        out_shape=(made(half, F32), made(half, F32)),
        in_specs=[smem(), smem(), vmem()],
        out_specs=(vmem(), vmem()),
        scratch_shapes=[pltpu.VMEM(item_factors.shape, F32)],
        compiler_params=params(),
        name="owners",
    )(place, asked, near(back))

    swap = [(u, u ^ 1) for u in range(rows)]
    back, give = lax.optimization_barrier((back, give))
    mate = lax.ppermute(give, "users", swap)
    umsg = pl.pallas_call(
        functools.partial(user_kernel, cap),
        out_shape=pltpu.HBM((owners, part + META, width), I16),
        in_specs=[vmem()],
        out_specs=vmem(),
        compiler_params=params(),
        name="users",
    )(near(back))
    keep, umsg = lax.optimization_barrier((keep, umsg))
    code = pl.pallas_call(
        chip_kernel,
        out_shape=made((held // 2 * tile + META, width), I16),
        in_specs=[vmem(), vmem()],
        out_specs=vmem(),
        compiler_params=params(),
        name="chip",
    )(near(keep), near(mate))
    ring = [
        lax.ppermute(code, "users", [(u, (u + 2 * k) % rows) for u in range(rows)])
        for k in range(1, 4)
    ]
    ugot = lax.all_to_all(umsg, "items", 0, 0, tiled=True)
    mine = pl.pallas_call(
        ring_kernel,
        out_shape=made(half, F32),
        in_specs=[smem()] + [vmem()] * 4,
        out_specs=vmem(),
        scratch_shapes=[pltpu.VMEM((4, tile, width), F32)],
        compiler_params=params(),
        name="ring",
    )(place, near(code), *[near(x) for x in ring])
    other = lax.ppermute(mine, "users", swap)
    item_total = pl.pallas_call(
        join_kernel,
        out_shape=jax.ShapeDtypeStruct(item_factors.shape, F32),
        in_specs=[smem(), vmem(), vmem()],
        out_specs=vmem(),
        compiler_params=params(),
        name="join",
    )(place, near(mine), near(other))
    user_total = pl.pallas_call(
        spread_kernel,
        out_shape=jax.ShapeDtypeStruct(user_factors.shape, F32),
        in_specs=[vmem()],
        out_specs=vmem(),
        compiler_params=params(),
        name="spread",
    )(near(ugot))
    return user_total, item_total


def solution(mesh):
    in_specs = (
        P("users", None, None),
        P("items", None, None),
        P(("users", "items"), None, None, None),
        P(("users", "items"), None, None, None),
        P(("users", "items"), None, None),
        P(("users", "items"), None),
        P(("users", "items"), None),
    )
    out_specs = (P("users", None, None), P("items", None, None))
    return jax.shard_map(body, mesh=mesh, in_specs=in_specs, out_specs=out_specs, check_vma=False)
```

```python
import functools

import jax
import jax.numpy as jnp
from jax import lax
from jax.experimental import pallas as pl
from jax.experimental.pallas import tpu as pltpu
from jax.sharding import PartitionSpec as P

F32 = jnp.float32
I16 = jnp.int16
I32 = jnp.int32
META = 16
STEP = 32
GROUP = 8
LIMIT = 32 * 1024 * 1024


def params():
    return pltpu.CompilerParams(vmem_limit_bytes=LIMIT)


def vmem():
    return pl.BlockSpec(memory_space=pltpu.VMEM)


def near(x):
    return pltpu.with_memory_space_constraint(x, pltpu.VMEM)


def far(x):
    return pltpu.with_memory_space_constraint(x, pltpu.HBM)


def made(shape, dtype):
    return pltpu.VMEM(shape, dtype)


def smem():
    return pl.BlockSpec(memory_space=pltpu.SMEM)


def encode(x):
    top = jnp.max(jnp.abs(x), axis=0, keepdims=True)
    expo = jnp.ceil(jnp.log2(jnp.maximum(top, 1e-30)) + 1e-4)
    scaled = x * jnp.exp2(14.99 - expo)
    return jnp.round(scaled).astype(I32).astype(I16), expo.astype(I32)


def decode(codes, expo):
    return codes.astype(I32).astype(F32) * jnp.exp2(expo.astype(F32) - 14.99)


def meta_rows(rows):
    width = rows[0].shape[1]
    index = lax.broadcasted_iota(I32, (META, width), 0)
    out = jnp.zeros((META, width), I32)
    for k, row in enumerate(rows):
        out = jnp.where(index == k, row, out)
    return out.astype(I16)


def dot(x, y, i, j):
    return lax.dot_general(x, y, (((i,), (j,)), ((), ())), preferred_element_type=F32)


def pick_kernel(ids, blocks, out):
    for i in range(out.shape[0]):
        for q in range(out.shape[1]):
            out[i, q] = blocks[jnp.maximum(ids[i, q], 0)]


def pair_kernel(pu, ps, conf, rate, users, slots, msg, ugrad, sgrad):
    step = pl.program_id(0)
    count = conf.shape[0]
    tile = conf.shape[1]

    @pl.when(step == 0)
    def _():
        ugrad[...] = jnp.zeros_like(ugrad)
        sgrad[...] = jnp.zeros_like(sgrad)

    for base in range(0, count, GROUP):
        picks = range(base, base + GROUP)
        bs = [pu[step * count + k] for k in picks]
        ss = [ps[step * count + k] for k in picks]
        lefts = [users[b] for b in bs]
        rights = [slots[s] for s in ss]
        scores = [dot(x, y, 1, 1) for x, y in zip(lefts, rights)]
        tiles = [
            (conf[k].astype(F32) * (score - rate[k].astype(F32)) * (1.0 / tile)).astype(jnp.bfloat16)
            for k, score in zip(picks, scores)
        ]
        by_user = [dot(w, y, 1, 0) for w, y in zip(tiles, rights)]
        by_slot = [dot(w, x, 0, 0) for w, x in zip(tiles, lefts)]
        for b, s, x, y in zip(bs, ss, by_user, by_slot):
            ugrad[b] += x
            sgrad[s] += y

    @pl.when(step == pl.num_programs(0) - 1)
    def _():
        owners = msg.shape[0]
        cap = sgrad.shape[0] // owners
        part = (msg.shape[1] - META) - cap * tile
        per = tile // part
        for i in range(owners):
            rows = []
            for q in range(cap):
                codes, expo = encode(sgrad[i * cap + q])
                msg[i, q * tile : (q + 1) * tile] = codes
                rows.append(expo)
            chunk = ugrad[i // per, (i % per) * part : (i % per + 1) * part]
            codes, expo = encode(chunk)
            msg[i, cap * tile : cap * tile + part] = codes
            rows.append(expo)
            msg[i, cap * tile + part :] = meta_rows(rows)


def item_kernel(place, ids, got, keep, give, acc):
    owners = got.shape[0]
    held, tile, width = acc.shape
    half = held // 2
    cap = ids.shape[1]
    part = (got.shape[1] - META) - cap * tile
    acc[...] = jnp.zeros_like(acc)
    for i in range(owners):
        meta = got[i, cap * tile + part :].astype(I32)
        for q in range(cap):
            block = ids[i, q]
            value = decode(got[i, q * tile : (q + 1) * tile], meta[q : q + 1])

            @pl.when(block >= 0)
            def _():
                acc[block] += value

    core = place[0]
    for r in range(half):
        keep[r] = acc[core * half + r]
        give[r] = acc[(1 - core) * half + r]


def user_kernel(cap, got, umsg):
    owners, rows, width = umsg.shape
    part = rows - META
    first = got.shape[1] - META - part
    total = jnp.zeros((part, width), F32)
    for i in range(owners):
        meta = got[i, first + part :].astype(I32)
        total += decode(got[i, first : first + part], meta[cap : cap + 1])
    codes, expo = encode(total)
    meta = meta_rows([expo])
    for i in range(owners):
        umsg[i, :part] = codes
        umsg[i, part:] = meta


def chip_kernel(keep, got, msg):
    half, tile, _ = keep.shape
    rows = []
    for r in range(half):
        codes, expo = encode(keep[r] + got[r])
        msg[r * tile : (r + 1) * tile] = codes
        rows.append(expo)
    msg[half * tile :] = meta_rows(rows)


def ring_kernel(place, own, one, two, three, out, stack):
    half, tile, _ = out.shape
    chips = stack.shape[0]
    for r in range(half):
        for k, ref in enumerate((own, one, two, three)):
            meta = ref[half * tile :].astype(I32)
            stack[k] = decode(ref[r * tile : (r + 1) * tile], meta[r : r + 1])
        total = stack[lax.rem(place[1], chips)]
        for y in range(1, chips):
            total += stack[lax.rem(place[1] + chips - y, chips)]
        out[r] = total


def join_kernel(place, mine, other, out, sems):
    half = mine.shape[0]
    core = place[0]
    copies = [
        pltpu.make_async_copy(mine, out.at[pl.ds(core * half, half)], sems.at[0]),
        pltpu.make_async_copy(other, out.at[pl.ds((1 - core) * half, half)], sems.at[1]),
    ]
    for copy in copies:
        copy.start()
    for copy in copies:
        copy.wait()


def spread_kernel(got, out):
    part = got.shape[1] - META
    per = out.shape[1] // part
    for r in range(got.shape[0]):
        meta = got[r, part:].astype(I32)
        out[r // per, (r % per) * part : (r % per + 1) * part] = decode(got[r, :part], meta[0:1])


def body(user_factors, item_factors, confidence, ratings, slot_blocks, pair_user, pair_slot):
    owners = lax.axis_size("items")
    rows = lax.axis_size("users")
    held, tile, width = item_factors.shape
    cap = slot_blocks.shape[2]
    count = pair_user.shape[1]
    part = user_factors.shape[0] * tile // owners
    step = min(STEP, count)
    row = lax.axis_index("users").astype(I32)
    place = jnp.stack([row & 1, row >> 1])
    wanted, place = lax.optimization_barrier((slot_blocks[0], place))

    asked = lax.all_to_all(wanted, "items", 0, 0, tiled=True)
    outgoing = pl.pallas_call(
        pick_kernel,
        out_shape=made((owners, cap, tile, width), item_factors.dtype),
        in_specs=[smem(), vmem()],
        out_specs=vmem(),
        compiler_params=params(),
        name="pick",
    )(asked, near(item_factors))
    incoming = lax.all_to_all(outgoing, "items", 0, 0, tiled=True)
    slots = near(incoming.reshape(owners * cap, tile, width))

    depth = cap * tile + part + META
    msg = pl.pallas_call(
        pair_kernel,
        out_shape=made((owners, depth, width), I16),
        grid_spec=pltpu.PrefetchScalarGridSpec(
            num_scalar_prefetch=2,
            grid=(count // step,),
            in_specs=[
                pl.BlockSpec((step, tile, tile), lambda p, *_: (p, 0, 0)),
                pl.BlockSpec((step, tile, tile), lambda p, *_: (p, 0, 0)),
                vmem(),
                vmem(),
            ],
            out_specs=vmem(),
            scratch_shapes=[
                pltpu.VMEM(user_factors.shape, F32),
                pltpu.VMEM((owners * cap, tile, width), F32),
            ],
        ),
        compiler_params=params(),
        name="pairs",
    )(pair_user[0], pair_slot[0], far(confidence[0]), far(ratings[0]), user_factors, slots)

    back = lax.all_to_all(msg, "items", 0, 0, tiled=True)
    half = (held // 2, tile, width)
    keep, give = pl.pallas_call(
        item_kernel,
        out_shape=(made(half, F32), made(half, F32)),
        in_specs=[smem(), smem(), vmem()],
        out_specs=(vmem(), vmem()),
        scratch_shapes=[pltpu.VMEM(item_factors.shape, F32)],
        compiler_params=params(),
        name="owners",
    )(place, asked, near(back))

    swap = [(u, u ^ 1) for u in range(rows)]
    back, give = lax.optimization_barrier((back, give))
    mate = lax.ppermute(give, "users", swap)
    umsg = pl.pallas_call(
        functools.partial(user_kernel, cap),
        out_shape=made((owners, part + META, width), I16),
        in_specs=[vmem()],
        out_specs=vmem(),
        compiler_params=params(),
        name="users",
    )(near(back))
    keep, umsg = lax.optimization_barrier((keep, umsg))
    code = pl.pallas_call(
        chip_kernel,
        out_shape=made((held // 2 * tile + META, width), I16),
        in_specs=[vmem(), vmem()],
        out_specs=vmem(),
        compiler_params=params(),
        name="chip",
    )(near(keep), near(mate))
    code, umsg = lax.optimization_barrier((code, umsg))
    ring = [
        lax.ppermute(code, "users", [(u, (u + 2 * k) % rows) for u in range(rows)])
        for k in range(1, 4)
    ]
    ugot = lax.all_to_all(umsg, "items", 0, 0, tiled=True)
    mine = pl.pallas_call(
        ring_kernel,
        out_shape=made(half, F32),
        in_specs=[smem()] + [vmem()] * 4,
        out_specs=vmem(),
        scratch_shapes=[pltpu.VMEM((4, tile, width), F32)],
        compiler_params=params(),
        name="ring",
    )(place, near(code), *[near(x) for x in ring])
    other = lax.ppermute(mine, "users", swap)
    item_total = pl.pallas_call(
        join_kernel,
        out_shape=pltpu.HBM(item_factors.shape, F32),
        in_specs=[smem(), vmem(), vmem()],
        out_specs=pl.BlockSpec(memory_space=pl.ANY),
        scratch_shapes=[pltpu.SemaphoreType.DMA((2,))],
        compiler_params=params(),
        name="join",
    )(place, near(mine), near(other))
    user_total = pl.pallas_call(
        spread_kernel,
        out_shape=jax.ShapeDtypeStruct(user_factors.shape, F32),
        in_specs=[vmem()],
        out_specs=vmem(),
        compiler_params=params(),
        name="spread",
    )(near(ugot))
    return user_total, item_total


def solution(mesh):
    in_specs = (
        P("users", None, None),
        P("items", None, None),
        P(("users", "items"), None, None, None),
        P(("users", "items"), None, None, None),
        P(("users", "items"), None, None),
        P(("users", "items"), None),
        P(("users", "items"), None),
    )
    out_specs = (P("users", None, None), P("items", None, None))
    return jax.shard_map(body, mesh=mesh, in_specs=in_specs, out_specs=out_specs, check_vma=False)
```
